32 devices in a mesh: grp: 2 (over y), seq: 16 (over z, x, core).
Axes of the slice: x: 2, y: 2, z: 4, core: 2. Of those that a mesh axis runs over, the one named last changes fastest.
Arguments:
- signal: bfloat16 [1024, 4096], P(None, ('grp', 'seq')), parts along dimension 1, may hold values from -6 to 6
- gate: bfloat16 [1024, 4096], P(None, ('grp', 'seq')), parts along dimension 1, may hold values from -6 to 6
- filter_taps: float32 [1024, 2048], P(None, 'seq'), may hold values from -2 to 2
- skip: float32 [1024], replicated, may hold values from -4 to 4
- up1_weight: bfloat16 [1024, 2048], replicated, may hold values from -0.1875 to 0.1875
- up1_bias: float32 [512], replicated, may hold values from -3 to 3
- res1_weight: bfloat16 [3584, 512], replicated, may hold values from -0.09375 to 0.09375
- res1_bias: float32 [512], replicated, may hold values from -3 to 3
- up2_weight: bfloat16 [512, 1024], replicated, may hold values from -0.25 to 0.25
- up2_bias: float32 [256], replicated, may hold values from -3 to 3
- res2_weight: bfloat16 [1792, 256], replicated, may hold values from -0.125 to 0.125
- res2_bias: float32 [256], replicated, may hold values from -3 to 3
- up3_weight: bfloat16 [256, 512], replicated, may hold values from -0.375 to 0.375
- up3_bias: float32 [128], replicated, may hold values from -3 to 3
- res3_weight: bfloat16 [896, 128], replicated, may hold values from -0.1875 to 0.1875
- res3_bias: float32 [128], replicated, may hold values from -3 to 3
Outputs:
- waveform_features: bfloat16 [262144, 128], P(('grp', 'seq')), parts along dimension 0
The draws below stay inside these ranges and needn't reach their ends.
There are 2 independent parts, one for each index of `grp`. The reference program is written for one: setup_inputs(seed, part) draws one part's arguments, and reference() takes and returns one part's arrays. A program takes and returns all parts, laid end to end along the dimension named above; an argument that names none is the same for every part. Nothing has to cross between parts.
All inputs are finite; a program needn't handle non-finite values.
Results may differ from the reference program's by a relative error of at most 0.018.
Values may be sent and summed in bfloat16 or wider, within the bound.
A program may use at most 128 MiB of HBM per device.

```python
import jax
import jax.numpy as jnp
from jax import lax

D = 1024
C1 = 512
C2 = 256
C3 = 128
TAPS = 7
STRIDE = 4
LEN = 2048


def draw_filter_taps(key, part):
    keys = jax.random.split(key, 6)
    lags = jnp.arange(LEN, dtype=jnp.float32)[None, :]
    slow_share = 0.5
    slow = jax.random.uniform(keys[0], (D, 1), jnp.float32) < slow_share
    fast_rate = jnp.exp(jax.random.uniform(keys[1], (D, 1), jnp.float32, jnp.log(1.0 / 50.0), jnp.log(1.0 / 30.0)))
    slow_rate = jnp.exp(jax.random.uniform(keys[2], (D, 1), jnp.float32, jnp.log(0.2 / LEN), jnp.log(2.0 / LEN)))
    rate = jnp.where(slow, slow_rate, fast_rate)
    amplitude = jnp.sqrt((1.0 - jnp.exp(-2.0 * rate)) / (1.0 - jnp.exp(-2.0 * rate * LEN)))
    places = jax.random.randint(keys[3], (3,), 1, LEN).astype(jnp.float32)
    factors = jax.random.uniform(keys[4], (D, 3), jnp.float32, 0.5, 0.8)
    envelope = jnp.exp(-rate * lags)
    for which in range(3):
        envelope = envelope * jnp.where(lags >= places[which], factors[:, which:which + 1], 1.0)
    noise = jnp.clip(jax.random.normal(keys[5], (D, LEN), jnp.float32), -4.0, 4.0)
    return amplitude * envelope * noise


def block_scale(own_key, shape, cuts, smallest, top_value):
    level = 1.0
    for axis_at, parts in cuts:
        draws = jax.random.uniform(jax.random.fold_in(jax.random.fold_in(own_key, 6), axis_at), (parts,), jnp.float32, smallest / len(cuts), top_value / len(cuts))
        level = level * jnp.repeat(jnp.exp(draws), shape[axis_at] // parts).reshape((-1,) + (1,) * (len(shape) - 1 - axis_at))
    return level


def normal_values(stream_key, extent, scale, most, cuts=(), kind=jnp.bfloat16):
    values = scale * jax.random.normal(stream_key, extent, jnp.float32)
    if cuts:
        values = values * block_scale(stream_key, extent, cuts, -0.22, 0.18)
    return jnp.clip(values, -most, most).astype(kind)


def setup_inputs(seed: int = 0, part: int = 0) -> dict:
    key_list = jax.random.split(jax.random.key(seed), 17)
    own_keys = jax.random.split(jax.random.fold_in(key_list[16], part), 17)
    signal = normal_values(own_keys[0], (D, LEN), 1.0, 6.0, ((1, 16),))
    gate = normal_values(own_keys[1], (D, LEN), 1.0, 6.0, ((1, 16),))
    filter_taps = draw_filter_taps(jax.random.fold_in(key_list[16], 71), part)
    skip = normal_values(key_list[3], (D,), 1.0, 4.0, (), jnp.float32)
    up1_weight = normal_values(key_list[4], (D, STRIDE * C1), D ** -0.5, 0.1875)
    up1_bias = normal_values(key_list[5], (C1,), 0.5, 3.0, (), jnp.float32)
    res1_weight = normal_values(key_list[6], (TAPS * C1, C1), (TAPS * C1) ** -0.5, 0.09375)
    res1_bias = normal_values(key_list[7], (C1,), 0.5, 3.0, (), jnp.float32)
    up2_weight = normal_values(key_list[8], (C1, STRIDE * C2), C1 ** -0.5, 0.25)
    up2_bias = normal_values(key_list[9], (C2,), 0.5, 3.0, (), jnp.float32)
    res2_weight = normal_values(key_list[10], (TAPS * C2, C2), (TAPS * C2) ** -0.5, 0.125)
    res2_bias = normal_values(key_list[11], (C2,), 0.5, 3.0, (), jnp.float32)
    up3_weight = normal_values(key_list[12], (C2, STRIDE * C3), C2 ** -0.5, 0.375)
    up3_bias = normal_values(key_list[13], (C3,), 0.5, 3.0, (), jnp.float32)
    res3_weight = normal_values(key_list[14], (TAPS * C3, C3), (TAPS * C3) ** -0.5, 0.1875)
    res3_bias = normal_values(key_list[15], (C3,), 0.5, 3.0, (), jnp.float32)
    return {"signal": signal, "gate": gate, "filter_taps": filter_taps, "skip": skip, "up1_weight": up1_weight, "up1_bias": up1_bias, "res1_weight": res1_weight, "res1_bias": res1_bias, "up2_weight": up2_weight, "up2_bias": up2_bias, "res2_weight": res2_weight, "res2_bias": res2_bias, "up3_weight": up3_weight, "up3_bias": up3_bias, "res3_weight": res3_weight, "res3_bias": res3_bias}


def residual_section(hidden, weight, bias):
    frames, width = hidden.shape
    half = TAPS // 2
    active = jax.nn.gelu(hidden.astype(jnp.float32), approximate=True).astype(jnp.bfloat16)
    padded = jnp.pad(active, ((half, half), (0, 0)))
    total = jnp.zeros((frames, width), jnp.float32)
    for offset in range(TAPS):
        total = total + jnp.dot(padded[offset:offset + frames], weight[offset * width:(offset + 1) * width], preferred_element_type=jnp.float32)
    return (hidden.astype(jnp.float32) + total + bias).astype(jnp.bfloat16)


def reference(signal, gate, filter_taps, skip, up1_weight, up1_bias, res1_weight, res1_bias, up2_weight, up2_bias, res2_weight, res2_bias, up3_weight, up3_bias, res3_weight, res3_bias):
    source = signal.astype(jnp.float32)
    length = 2 * LEN
    spectrum = jnp.fft.rfft(source, n=length, axis=1) * jnp.fft.rfft(filter_taps, n=length, axis=1)
    conv = jnp.fft.irfft(spectrum, n=length, axis=1)[:, :LEN]
    mixed = (conv + skip[:, None] * source).astype(jnp.bfloat16)
    latent = (gate.astype(jnp.float32) * mixed.astype(jnp.float32)).astype(jnp.bfloat16)
    wide = lax.dot_general(latent, up1_weight, (((0,), (0,)), ((), ())), preferred_element_type=jnp.float32)
    hidden = (wide.reshape(-1, C1) + up1_bias).astype(jnp.bfloat16)
    current = residual_section(hidden, res1_weight, res1_bias)
    wide = jnp.dot(current, up2_weight, preferred_element_type=jnp.float32)
    hidden = (wide.reshape(-1, C2) + up2_bias).astype(jnp.bfloat16)
    current = residual_section(hidden, res2_weight, res2_bias)
    wide = jnp.dot(current, up3_weight, preferred_element_type=jnp.float32)
    hidden = (wide.reshape(-1, C3) + up3_bias).astype(jnp.bfloat16)
    return residual_section(hidden, res3_weight, res3_bias)
```

```python
import functools
import math

import jax
import jax.numpy as jnp
from jax import lax
from jax.experimental import pallas as pl
from jax.experimental.pallas import tpu as pltpu
from jax.sharding import PartitionSpec as P

HIGHEST = lax.Precision.HIGHEST


def angle_table(rows, cols, modulus):
    product = (
        lax.broadcasted_iota(jnp.int32, (rows, cols), 0)
        * lax.broadcasted_iota(jnp.int32, (rows, cols), 1)
        % modulus
    )
    theta = product.astype(jnp.float32) * (2.0 * math.pi / modulus)
    return (jnp.cos(theta), jnp.sin(theta))


def forward(values, tables):
    outer_cos, outer_sin, twist_cos, twist_sin, inner_cos, inner_sin = tables
    first_re = jnp.einsum("kn,cnm->ckm", outer_cos, values, precision=HIGHEST)
    first_im = -jnp.einsum("kn,cnm->ckm", outer_sin, values, precision=HIGHEST)
    turned_re = first_re * twist_cos + first_im * twist_sin
    turned_im = first_im * twist_cos - first_re * twist_sin
    spec_re = jnp.einsum("ckm,mj->ckj", turned_re, inner_cos, precision=HIGHEST) + jnp.einsum(
        "ckm,mj->ckj", turned_im, inner_sin, precision=HIGHEST
    )
    spec_im = jnp.einsum("ckm,mj->ckj", turned_im, inner_cos, precision=HIGHEST) - jnp.einsum(
        "ckm,mj->ckj", turned_re, inner_sin, precision=HIGHEST
    )
    return (spec_re, spec_im)


def inverse(spec_re, spec_im, tables, modulus):
    outer_cos, outer_sin, twist_cos, twist_sin, inner_cos, inner_sin = tables
    back_re = jnp.einsum("ckm,mj->ckj", spec_re, inner_cos, precision=HIGHEST) - jnp.einsum(
        "ckm,mj->ckj", spec_im, inner_sin, precision=HIGHEST
    )
    back_im = jnp.einsum("ckm,mj->ckj", spec_im, inner_cos, precision=HIGHEST) + jnp.einsum(
        "ckm,mj->ckj", spec_re, inner_sin, precision=HIGHEST
    )
    turned_re = back_re * twist_cos - back_im * twist_sin
    turned_im = back_im * twist_cos + back_re * twist_sin
    result = jnp.einsum("kn,ckm->cnm", outer_cos, turned_re, precision=HIGHEST) - jnp.einsum(
        "kn,ckm->cnm", outer_sin, turned_im, precision=HIGHEST
    )
    return result / modulus


def gelu(v):
    return 0.5 * v * (1.0 + jnp.tanh(0.7978845608 * (v + 0.044715 * (v * v * v))))


def decoder_kernel(
    frames, edge, lat_ref, b1_ref, rb1_ref, b2_ref, rb2_ref, b3_ref, rb3_ref, edges_ref,
    up1_hbm, res1_hbm, up2_hbm, res2_hbm, up3_hbm, res3_hbm,
    out_ref,
    up1, res1, up2, res2, up3, res3, act1, hid1, x1, act2, hid2, x2, act3, hid3, fine, sems,
):
    copies = [
        pltpu.make_async_copy(src, dst, sems.at[i])
        for i, (src, dst) in enumerate(
            [(up1_hbm, up1), (res1_hbm, res1), (up2_hbm, up2), (res2_hbm, res2), (up3_hbm, up3), (res3_hbm, res3)]
        )
    ]
    for copy in copies:
        copy.start()
    rows = frames + edge
    w1, w2, w3 = b1_ref.shape[1], b2_ref.shape[1], b3_ref.shape[1]
    at = lax.broadcasted_iota(jnp.int32, (rows, 1), 0)
    keep_first = edges_ref[0:1, 0:1]
    keep_last = edges_ref[1:2, 0:1]
    before_scale = jnp.where(at == 0, keep_first, 1.0)
    after_scale = jnp.where(at == frames - 1, keep_last, 1.0)

    def before(v):
        return (pltpu.roll(v, 1, 0) * before_scale).astype(jnp.bfloat16)

    def after(v):
        return (pltpu.roll(v, rows - 1, 0) * after_scale).astype(jnp.bfloat16)

    def dot(a, b):
        return jnp.dot(a, b, preferred_element_type=jnp.float32)

    copies[0].wait()
    for k in range(4):
        h = (dot(lat_ref[...], up1[:, k * w1 : (k + 1) * w1]) + b1_ref[...]).astype(jnp.bfloat16)
        hid1[:, k * w1 : (k + 1) * w1] = h
        a = gelu(h.astype(jnp.float32))
        act1[:, (3 + k) * w1 : (4 + k) * w1] = a.astype(jnp.bfloat16)
        if k > 0:
            act1[:, (k - 1) * w1 : k * w1] = before(a)
        if k < 3:
            act1[:, (7 + k) * w1 : (8 + k) * w1] = after(a)
    copies[1].wait()
    for k in range(4):
        y = dot(act1[:, k * w1 : (k + 7) * w1], res1[...])
        y = y + hid1[:, k * w1 : (k + 1) * w1].astype(jnp.float32) + rb1_ref[...]
        x1[k * rows : (k + 1) * rows, :] = y.astype(jnp.bfloat16)

    def section(blocks, x, up, up_bias, hid, act, w, group):
        @pl.loop(0, blocks)
        def _(b):
            here = pl.ds(pl.multiple_of(b * rows, 16), rows)
            prev = pl.ds(pl.multiple_of(lax.rem(b + blocks - 1, blocks) * rows, 16), rows)
            nxt = pl.ds(pl.multiple_of(lax.rem(b + 1, blocks) * rows, 16), rows)
            h = (dot(x[here, :], up[...]) + jnp.concatenate([up_bias[...]] * 4, axis=1)).astype(jnp.bfloat16)
            hid[here, :] = h
            a = gelu(h.astype(jnp.float32))
            low = a.astype(jnp.bfloat16)
            act[here, 3 * w : 7 * w] = low

            @pl.when(b < blocks - 1)
            def _():
                act[nxt, 0 : 3 * w] = low[:, w:]

            @pl.when(b == blocks - 1)
            def _():
                act[0:rows, 0 : 3 * w] = before(a[:, w:])

            @pl.when(b > 0)
            def _():
                act[prev, 7 * w : 10 * w] = low[:, : 3 * w]

            @pl.when(b == 0)
            def _():
                act[(blocks - 1) * rows : blocks * rows, 7 * w : 10 * w] = after(a[:, : 3 * w])

    copies[2].wait()
    section(4, x1, up2, b2_ref, hid2, act2, w2, 1)
    copies[3].wait()

    for k in range(4):
        @pl.loop(0, 2)
        def _(b):
            here = pl.ds(pl.multiple_of(b * 2 * rows, 16), 2 * rows)
            y = dot(act2[here, k * w2 : (k + 7) * w2], res2[...])
            y = (y + hid2[here, k * w2 : (k + 1) * w2].astype(jnp.float32) + rb2_ref[...]).astype(jnp.bfloat16)
            for i in range(2):
                x2[pl.ds(pl.multiple_of((b * 8 + i * 4 + k) * rows, 16), rows), :] = y[i * rows : (i + 1) * rows]

    copies[4].wait()
    section(16, x2, up3, b3_ref, hid3, act3, w3, 1)
    copies[5].wait()
    rb3 = jnp.concatenate([rb3_ref[...]] * 2, axis=1)

    @pl.loop(0, 16)
    def _(b):
        here = pl.ds(pl.multiple_of(b * rows, 16), frames)
        for k in range(2):
            y = dot(act3[here, 2 * k * w3 : (2 * k + 8) * w3], res3[...])
            y = y + hid3[here, 2 * k * w3 : (2 * k + 2) * w3].astype(jnp.float32) + rb3
            for i in range(2):
                fine[pl.ds(b * 4 + 2 * k + i, frames, stride=64), :] = y[:, i * w3 : (i + 1) * w3]

    @pl.loop(0, 16)
    def _(b):
        here = pl.ds(pl.multiple_of(b * 4 * frames, 16), 4 * frames)
        out_ref[here, :] = fine[here, :].astype(jnp.bfloat16)


def decode(lat, first, last, weights):
    (up1, b1, res1, rb1, up2, b2, res2, rb2, up3, b3, res3, rb3) = weights
    rows = lat.shape[0]
    edge = 16
    frames = rows - edge
    w1, w2, w3 = b1.shape[0], b2.shape[0], b3.shape[0]
    zero = jnp.zeros((w3, w3), res3.dtype)
    pair = jnp.concatenate(
        [jnp.concatenate([res3, zero], axis=0), jnp.concatenate([zero, res3], axis=0)], axis=1
    )
    edges = jnp.broadcast_to(
        jnp.stack([jnp.where(first, 0.0, 1.0), jnp.where(last, 0.0, 1.0)] * 4)[:, None], (8, 128)
    ).astype(jnp.float32)
    row = lambda v: v[None, :]
    vm = pl.BlockSpec(memory_space=pltpu.VMEM)
    hb = pl.BlockSpec(memory_space=pl.ANY)
    bf = jnp.bfloat16
    return pl.pallas_call(
        functools.partial(decoder_kernel, frames, edge),
        out_shape=jax.ShapeDtypeStruct((frames * 64, w3), bf),
        in_specs=[vm] * 8 + [hb] * 6,
        out_specs=vm,
        scratch_shapes=[
            pltpu.VMEM(up1.shape, bf),
            pltpu.VMEM(res1.shape, bf),
            pltpu.VMEM(up2.shape, bf),
            pltpu.VMEM(res2.shape, bf),
            pltpu.VMEM(up3.shape, bf),
            pltpu.VMEM(pair.shape, bf),
            pltpu.VMEM((rows, 10 * w1), bf),
            pltpu.VMEM((rows, 4 * w1), bf),
            pltpu.VMEM((4 * rows, w1), bf),
            pltpu.VMEM((4 * rows, 10 * w2), bf),
            pltpu.VMEM((4 * rows, 4 * w2), bf),
            pltpu.VMEM((16 * rows, w2), bf),
            pltpu.VMEM((16 * rows, 10 * w3), bf),
            pltpu.VMEM((16 * rows, 4 * w3), bf),
            pltpu.VMEM((64 * frames, w3), jnp.float32),
            pltpu.SemaphoreType.DMA((6,)),
        ],
        compiler_params=pltpu.CompilerParams(vmem_limit_bytes=60 * 1024 * 1024),
    )(lat, row(b1), row(rb1), row(b2), row(rb2), row(b3), row(rb3), edges, up1, res1, up2, res2, up3, pair)


def body(
    signal,
    gate,
    filter_taps,
    skip,
    up1_weight,
    up1_bias,
    res1_weight,
    res1_bias,
    up2_weight,
    up2_bias,
    res2_weight,
    res2_bias,
    up3_weight,
    up3_bias,
    res3_weight,
    res3_bias,
):
    parts = lax.axis_size("seq")
    frames = signal.shape[1]
    chans = signal.shape[0] // parts
    modulus = 2 * parts * frames
    source, taps = (
        lax.all_to_all(
            signal.astype(jnp.float32).astype(jnp.bfloat16),
            "seq",
            split_axis=0,
            concat_axis=1,
            tiled=True,
        ).astype(jnp.float32),
        lax.all_to_all(
            filter_taps.astype(jnp.bfloat16), "seq", split_axis=0, concat_axis=1, tiled=True
        ).astype(filter_taps.dtype),
    )
    my_skip = lax.dynamic_slice_in_dim(skip, lax.axis_index("seq") * chans, chans, 0)
    tables = (
        angle_table(2 * parts, parts, 2 * parts)
        + angle_table(2 * parts, frames, modulus)
        + angle_table(frames, frames, frames)
    )
    sig_re, sig_im = forward(source.reshape(chans, parts, frames), tables)
    fil_re, fil_im = forward(taps.reshape(chans, parts, frames), tables)
    prod_re = sig_re * fil_re - sig_im * fil_im
    prod_im = sig_re * fil_im + sig_im * fil_re
    conv = inverse(prod_re, prod_im, tables, modulus).reshape(chans, parts * frames)
    mixed = (conv + my_skip[:, None] * source).astype(jnp.bfloat16)
    arrived = lax.all_to_all(mixed, "seq", split_axis=1, concat_axis=0, tiled=True)
    latent = (gate.astype(jnp.float32) * arrived.astype(jnp.float32)).astype(jnp.bfloat16)
    count = parts
    up = [(i, i + 1) for i in range(count - 1)]
    down = [(i + 1, i) for i in range(count - 1)]
    prev = lax.ppermute(latent[:, -1], "seq", up)
    nxt = lax.ppermute(latent[:, 0], "seq", down)
    at = lax.broadcasted_iota(jnp.int32, (16, 1), 0)
    halo = jnp.where(at < 8, nxt[None, :], prev[None, :])
    lat = jnp.concatenate([latent.T, halo], axis=0)
    me = lax.axis_index("seq")
    weights = (
        up1_weight, up1_bias, res1_weight, res1_bias, up2_weight, up2_bias,
        res2_weight, res2_bias, up3_weight, up3_bias, res3_weight, res3_bias,
    )
    return decode(lat, me == 0, me == parts - 1, weights)


def solution(mesh):
    placed = (
        P(None, ("grp", "seq")),
        P(None, ("grp", "seq")),
        P(None, "seq"),
        P(),
        P(),
        P(),
        P(),
        P(),
        P(),
        P(),
        P(),
        P(),
        P(),
        P(),
        P(),
        P(),
    )
    return jax.shard_map(
        body, mesh=mesh, in_specs=placed, out_specs=P(("grp", "seq"), None), check_vma=False
    )
```

```python
import functools
import math

import jax
import jax.numpy as jnp
from jax import lax
from jax.experimental import pallas as pl
from jax.experimental.pallas import tpu as pltpu
from jax.sharding import PartitionSpec as P

HIGHEST = lax.Precision.HIGHEST


def angle_table(rows, cols, modulus):
    product = (
        lax.broadcasted_iota(jnp.int32, (rows, cols), 0)
        * lax.broadcasted_iota(jnp.int32, (rows, cols), 1)
        % modulus
    )
    theta = product.astype(jnp.float32) * (2.0 * math.pi / modulus)
    return (jnp.cos(theta), jnp.sin(theta))


def forward(values, tables):
    outer_cos, outer_sin, twist_cos, twist_sin, inner_cos, inner_sin = tables
    first_re = jnp.einsum("kn,cnm->ckm", outer_cos, values, precision=HIGHEST)
    first_im = -jnp.einsum("kn,cnm->ckm", outer_sin, values, precision=HIGHEST)
    turned_re = first_re * twist_cos + first_im * twist_sin
    turned_im = first_im * twist_cos - first_re * twist_sin
    spec_re = jnp.einsum("ckm,mj->ckj", turned_re, inner_cos, precision=HIGHEST) + jnp.einsum(
        "ckm,mj->ckj", turned_im, inner_sin, precision=HIGHEST
    )
    spec_im = jnp.einsum("ckm,mj->ckj", turned_im, inner_cos, precision=HIGHEST) - jnp.einsum(
        "ckm,mj->ckj", turned_re, inner_sin, precision=HIGHEST
    )
    return (spec_re, spec_im)


def inverse(spec_re, spec_im, tables, modulus):
    outer_cos, outer_sin, twist_cos, twist_sin, inner_cos, inner_sin = tables
    back_re = jnp.einsum("ckm,mj->ckj", spec_re, inner_cos, precision=HIGHEST) - jnp.einsum(
        "ckm,mj->ckj", spec_im, inner_sin, precision=HIGHEST
    )
    back_im = jnp.einsum("ckm,mj->ckj", spec_im, inner_cos, precision=HIGHEST) + jnp.einsum(
        "ckm,mj->ckj", spec_re, inner_sin, precision=HIGHEST
    )
    turned_re = back_re * twist_cos - back_im * twist_sin
    turned_im = back_im * twist_cos + back_re * twist_sin
    result = jnp.einsum("kn,ckm->cnm", outer_cos, turned_re, precision=HIGHEST) - jnp.einsum(
        "kn,ckm->cnm", outer_sin, turned_im, precision=HIGHEST
    )
    return result / modulus


def gelu(v):
    return 0.5 * v * (1.0 + jnp.tanh(0.7978845608 * (v + 0.044715 * (v * v * v))))


def decoder_kernel(
    frames, edge, lat_ref, b1_ref, rb1_ref, b2_ref, rb2_ref, b3_ref, rb3_ref, edges_ref,
    up1_hbm, res1_hbm, up2_hbm, res2_hbm, up3_hbm, res3_hbm,
    out_ref,
    up1, res1, up2, res2, up3, res3, act1, hid1, x1, act2, hid2, x2, act3, hid3, fine, sems,
):
    copies = [
        pltpu.make_async_copy(src, dst, sems.at[i])
        for i, (src, dst) in enumerate(
            [(up1_hbm, up1), (res1_hbm, res1), (up2_hbm, up2), (res2_hbm, res2), (up3_hbm, up3), (res3_hbm, res3)]
        )
    ]
    for copy in copies:
        copy.start()
    rows = frames + edge
    w1, w2, w3 = b1_ref.shape[1], b2_ref.shape[1], b3_ref.shape[1]
    at = lax.broadcasted_iota(jnp.int32, (rows, 1), 0)
    keep_first = edges_ref[0:1, 0:1]
    keep_last = edges_ref[1:2, 0:1]
    before_scale = jnp.where(at == 0, keep_first, 1.0)
    after_scale = jnp.where(at == frames - 1, keep_last, 1.0)

    def before(v):
        return (pltpu.roll(v, 1, 0) * before_scale).astype(jnp.bfloat16)

    def after(v):
        return (pltpu.roll(v, rows - 1, 0) * after_scale).astype(jnp.bfloat16)

    def dot(a, b):
        return jnp.dot(a, b, preferred_element_type=jnp.float32)

    copies[0].wait()
    for k in range(4):
        h = (dot(lat_ref[...], up1[:, k * w1 : (k + 1) * w1]) + b1_ref[...]).astype(jnp.bfloat16)
        hid1[:, k * w1 : (k + 1) * w1] = h
        a = gelu(h.astype(jnp.float32))
        act1[:, (3 + k) * w1 : (4 + k) * w1] = a.astype(jnp.bfloat16)
        if k > 0:
            act1[:, (k - 1) * w1 : k * w1] = before(a)
        if k < 3:
            act1[:, (7 + k) * w1 : (8 + k) * w1] = after(a)
    copies[1].wait()
    for k in range(4):
        y = dot(act1[:, k * w1 : (k + 7) * w1], res1[...])
        y = y + hid1[:, k * w1 : (k + 1) * w1].astype(jnp.float32) + rb1_ref[...]
        x1[k * rows : (k + 1) * rows, :] = y.astype(jnp.bfloat16)

    def section(blocks, x, up, up_bias, hid, act, w, group):
        @pl.loop(0, blocks)
        def _(b):
            here = pl.ds(pl.multiple_of(b * rows, 16), rows)
            prev = pl.ds(pl.multiple_of(lax.rem(b + blocks - 1, blocks) * rows, 16), rows)
            nxt = pl.ds(pl.multiple_of(lax.rem(b + 1, blocks) * rows, 16), rows)
            h = (dot(x[here, :], up[...]) + jnp.concatenate([up_bias[...]] * 4, axis=1)).astype(jnp.bfloat16)
            hid[here, :] = h
            a = gelu(h.astype(jnp.float32))
            low = a.astype(jnp.bfloat16)
            act[here, 3 * w : 7 * w] = low

            @pl.when(b < blocks - 1)
            def _():
                act[nxt, 0 : 3 * w] = low[:, w:]

            @pl.when(b == blocks - 1)
            def _():
                act[0:rows, 0 : 3 * w] = before(a[:, w:])

            @pl.when(b > 0)
            def _():
                act[prev, 7 * w : 10 * w] = low[:, : 3 * w]

            @pl.when(b == 0)
            def _():
                act[(blocks - 1) * rows : blocks * rows, 7 * w : 10 * w] = after(a[:, : 3 * w])

    copies[2].wait()
    section(4, x1, up2, b2_ref, hid2, act2, w2, 1)
    copies[3].wait()

    for k in range(4):
        @pl.loop(0, 2)
        def _(b):
            here = pl.ds(pl.multiple_of(b * 2 * rows, 16), 2 * rows)
            y = dot(act2[here, k * w2 : (k + 7) * w2], res2[...])
            y = (y + hid2[here, k * w2 : (k + 1) * w2].astype(jnp.float32) + rb2_ref[...]).astype(jnp.bfloat16)
            for i in range(2):
                x2[pl.ds(pl.multiple_of((b * 8 + i * 4 + k) * rows, 16), rows), :] = y[i * rows : (i + 1) * rows]

    copies[4].wait()
    section(16, x2, up3, b3_ref, hid3, act3, w3, 1)
    copies[5].wait()
    rb3 = jnp.concatenate([rb3_ref[...]] * 2, axis=1)

    @pl.loop(0, 16)
    def _(b):
        here = pl.ds(pl.multiple_of(b * rows, 16), frames)
        for k in range(2):
            y = dot(act3[here, 2 * k * w3 : (2 * k + 8) * w3], res3[...])
            y = y + hid3[here, 2 * k * w3 : (2 * k + 2) * w3].astype(jnp.float32) + rb3
            for i in range(2):
                fine[pl.ds(b * 4 + 2 * k + i, frames, stride=64), :] = y[:, i * w3 : (i + 1) * w3]

    @pl.loop(0, 16)
    def _(b):
        here = pl.ds(pl.multiple_of(b * 4 * frames, 16), 4 * frames)
        out_ref[here, :] = fine[here, :].astype(jnp.bfloat16)


def decode(lat, first, last, weights):
    (up1, b1, res1, rb1, up2, b2, res2, rb2, up3, b3, res3, rb3) = weights
    rows = lat.shape[0]
    edge = 16
    frames = rows - edge
    w1, w2, w3 = b1.shape[0], b2.shape[0], b3.shape[0]
    zero = jnp.zeros((w3, w3), res3.dtype)
    pair = jnp.concatenate(
        [jnp.concatenate([res3, zero], axis=0), jnp.concatenate([zero, res3], axis=0)], axis=1
    )
    edges = jnp.broadcast_to(
        jnp.stack([jnp.where(first, 0.0, 1.0), jnp.where(last, 0.0, 1.0)] * 4)[:, None], (8, 128)
    ).astype(jnp.float32)
    row = lambda v: v[None, :]
    vm = pl.BlockSpec(memory_space=pltpu.VMEM)
    hb = pl.BlockSpec(memory_space=pl.ANY)
    bf = jnp.bfloat16
    return pl.pallas_call(
        functools.partial(decoder_kernel, frames, edge),
        out_shape=jax.ShapeDtypeStruct((frames * 64, w3), bf),
        in_specs=[vm] * 8 + [hb] * 6,
        out_specs=vm,
        scratch_shapes=[
            pltpu.VMEM(up1.shape, bf),
            pltpu.VMEM(res1.shape, bf),
            pltpu.VMEM(up2.shape, bf),
            pltpu.VMEM(res2.shape, bf),
            pltpu.VMEM(up3.shape, bf),
            pltpu.VMEM(pair.shape, bf),
            pltpu.VMEM((rows, 10 * w1), bf),
            pltpu.VMEM((rows, 4 * w1), bf),
            pltpu.VMEM((4 * rows, w1), bf),
            pltpu.VMEM((4 * rows, 10 * w2), bf),
            pltpu.VMEM((4 * rows, 4 * w2), bf),
            pltpu.VMEM((16 * rows, w2), bf),
            pltpu.VMEM((16 * rows, 10 * w3), bf),
            pltpu.VMEM((16 * rows, 4 * w3), bf),
            pltpu.VMEM((64 * frames, w3), jnp.float32),
            pltpu.SemaphoreType.DMA((6,)),
        ],
        compiler_params=pltpu.CompilerParams(vmem_limit_bytes=60 * 1024 * 1024),
    )(lat, row(b1), row(rb1), row(b2), row(rb2), row(b3), row(rb3), edges, up1, res1, up2, res2, up3, pair)


def mix_kernel(
    groups, parts, nc, sig_ref, gate_ref, tap_ref, lat_ref,
    sig_in, tap_in, mix_out, mix_in, tap_wide, sig_wide, mix_wide, line, edge_next, edge_prev,
    sig_send, sig_recv, tap_send, tap_recv, mix_send, mix_recv, edge_send, edge_recv,
):
    g, s = lax.axis_index("grp"), lax.axis_index("seq")
    total = groups * parts
    me = g * parts + s
    frames = sig_ref.shape[1]

    def place(index):
        return (index // parts, lax.rem(index, parts))

    def rows(index):
        return pl.ds(pl.multiple_of(index * nc, 16), nc)

    def sig_copy(peer, slot):
        return pltpu.make_async_remote_copy(
            sig_ref.at[rows(peer)], sig_in.at[rows(slot)], sig_send.at[peer], sig_recv.at[slot],
            device_id=place(peer), device_id_type=pl.DeviceIdType.MESH,
        )

    def tap_copy(peer, slot):
        return pltpu.make_async_remote_copy(
            tap_ref.at[rows(g * parts + peer)], tap_in.at[rows(slot)], tap_send.at[peer], tap_recv.at[slot],
            device_id=(g, peer), device_id_type=pl.DeviceIdType.MESH,
        )

    def mix_copy(peer, slot):
        return pltpu.make_async_remote_copy(
            mix_out.at[rows(peer)], mix_in.at[rows(slot)], mix_send.at[peer], mix_recv.at[slot],
            device_id=place(peer), device_id_type=pl.DeviceIdType.MESH,
        )

    barrier = pltpu.get_barrier_semaphore()

    @pl.loop(1, total)
    def _(step):
        pl.semaphore_signal(
            barrier, inc=1, device_id=place(lax.rem(me + step, total)), device_id_type=pl.DeviceIdType.MESH
        )

    pl.semaphore_wait(barrier, total - 1)

    @pl.loop(1, parts)
    def _(step):
        tap_copy(lax.rem(s + step, parts), s).start()

    @pl.loop(1, total)
    def _(step):
        sig_copy(lax.rem(me + step, total), me).start()

    sig_in[rows(me), :] = sig_ref[rows(me), :]
    tap_in[rows(s), :] = tap_ref[rows(me), :]
    line[...] = jnp.zeros_like(line)

    @pl.loop(1, parts)
    def _(step):
        tap_copy(s, lax.rem(s + step, parts)).wait_recv()

    tap_wide[...] = tap_in[...].astype(jnp.float32)

    @pl.loop(1, total)
    def _(step):
        sig_copy(me, lax.rem(me + step, total)).wait_recv()

    sig_wide[...] = sig_in[...].astype(jnp.float32)
    below = lax.broadcasted_iota(jnp.int32, (frames, frames), 1) >= lax.broadcasted_iota(
        jnp.int32, (frames, frames), 0
    )

    @pl.loop(0, nc)
    def _(c):
        for part in range(groups):
            line[(2 * part + 1) * parts : (2 * part + 2) * parts, :] = sig_wide[
                pl.ds(part * parts * nc + c, parts, stride=nc), :
            ]
        acc = jnp.zeros((total, frames), jnp.float32)
        last = jnp.zeros((frames, frames), jnp.float32)
        for pair in range(0, parts, 2):
            tiles, shifted = [], []
            for d in (pair, pair + 1):
                row = tap_wide[pl.ds(d * nc + c, 1), :]
                turned = pltpu.roll(jnp.broadcast_to(row, (frames, frames)), 0, 1, stride=1, stride_axis=0)
                tiles.append(jnp.where(below, turned, last).astype(jnp.bfloat16))
                last = turned
                shifted.append(
                    jnp.concatenate(
                        [
                            line[(2 * part + 1) * parts - d : (2 * part + 2) * parts - d, :]
                            for part in range(groups)
                        ],
                        axis=0,
                    ).astype(jnp.bfloat16)
                )
            acc = acc + jnp.dot(
                jnp.concatenate(shifted, axis=1),
                jnp.concatenate(tiles, axis=0),
                preferred_element_type=jnp.float32,
            )
        mix_wide[pl.ds(c, total, stride=nc), :] = acc

    mix_out[...] = mix_wide[...].astype(jnp.bfloat16)

    @pl.loop(1, total)
    def _(step):
        mix_copy(lax.rem(me + step, total), me).start()

    mix_in[rows(me), :] = mix_out[rows(me), :]

    @pl.loop(1, total)
    def _(step):
        mix_copy(me, lax.rem(me + step, total)).wait_recv()

    latent = mix_in[...].astype(jnp.float32) * gate_ref[...].astype(jnp.float32)
    lat_ref[0:frames, :] = latent.T.astype(jnp.bfloat16)

    nxt, prv = lax.rem(s + 1, parts), lax.rem(s + parts - 1, parts)
    down = pltpu.make_async_remote_copy(
        lat_ref.at[pl.ds(0, 16)], edge_next, edge_send.at[0], edge_recv.at[0],
        device_id=(g, prv), device_id_type=pl.DeviceIdType.MESH,
    )
    up = pltpu.make_async_remote_copy(
        lat_ref.at[pl.ds(frames - 16, 16)], edge_prev, edge_send.at[1], edge_recv.at[1],
        device_id=(g, nxt), device_id_type=pl.DeviceIdType.MESH,
    )
    down.start()
    up.start()

    @pl.loop(1, parts)
    def _(step):
        tap_copy(lax.rem(s + step, parts), s).wait_send()

    @pl.loop(1, total)
    def _(step):
        sig_copy(lax.rem(me + step, total), me).wait_send()
        mix_copy(lax.rem(me + step, total), me).wait_send()

    down.wait()
    up.wait()
    at = lax.broadcasted_iota(jnp.int32, (16, 1), 0)
    lat_ref[frames : frames + 16, :] = jnp.where(
        at < 8, edge_next[...].astype(jnp.float32), edge_prev[...].astype(jnp.float32)
    ).astype(jnp.bfloat16)


def mix(signal, gate, taps, groups, parts):
    chans, frames = signal.shape
    total = groups * parts
    nc = chans // total
    vm = pl.BlockSpec(memory_space=pltpu.VMEM)
    bf, f32 = jnp.bfloat16, jnp.float32
    dma = pltpu.SemaphoreType.DMA
    return pl.pallas_call(
        functools.partial(mix_kernel, groups, parts, nc),
        out_shape=jax.ShapeDtypeStruct((frames + 16, chans), bf),
        in_specs=[vm] * 3,
        out_specs=vm,
        scratch_shapes=[
            pltpu.VMEM((chans, frames), bf),
            pltpu.VMEM((parts * nc, frames), bf),
            pltpu.VMEM((chans, frames), bf),
            pltpu.VMEM((chans, frames), bf),
            pltpu.VMEM((parts * nc, frames), f32),
            pltpu.VMEM((chans, frames), f32),
            pltpu.VMEM((chans, frames), f32),
            pltpu.VMEM((groups * 2 * parts, frames), f32),
            pltpu.VMEM((16, chans), bf),
            pltpu.VMEM((16, chans), bf),
            dma((total,)), dma((total,)), dma((parts,)), dma((parts,)),
            dma((total,)), dma((total,)), dma((2,)), dma((2,)),
        ],
        compiler_params=pltpu.CompilerParams(
            collective_id=0, has_side_effects=True, vmem_limit_bytes=40 * 1024 * 1024
        ),
    )(signal, gate, taps)


def transformed(signal, gate, filter_taps, skip):
    parts = lax.axis_size("seq")
    frames = signal.shape[1]
    chans = signal.shape[0] // parts
    modulus = 2 * parts * frames
    source, taps = (
        lax.all_to_all(
            signal.astype(jnp.float32).astype(jnp.bfloat16),
            "seq",
            split_axis=0,
            concat_axis=1,
            tiled=True,
        ).astype(jnp.float32),
        lax.all_to_all(
            filter_taps.astype(jnp.bfloat16), "seq", split_axis=0, concat_axis=1, tiled=True
        ).astype(filter_taps.dtype),
    )
    my_skip = lax.dynamic_slice_in_dim(skip, lax.axis_index("seq") * chans, chans, 0)
    tables = (
        angle_table(2 * parts, parts, 2 * parts)
        + angle_table(2 * parts, frames, modulus)
        + angle_table(frames, frames, frames)
    )
    sig_re, sig_im = forward(source.reshape(chans, parts, frames), tables)
    fil_re, fil_im = forward(taps.reshape(chans, parts, frames), tables)
    prod_re = sig_re * fil_re - sig_im * fil_im
    prod_im = sig_re * fil_im + sig_im * fil_re
    conv = inverse(prod_re, prod_im, tables, modulus).reshape(chans, parts * frames)
    mixed = (conv + my_skip[:, None] * source).astype(jnp.bfloat16)
    arrived = lax.all_to_all(mixed, "seq", split_axis=1, concat_axis=0, tiled=True)
    latent = (gate.astype(jnp.float32) * arrived.astype(jnp.float32)).astype(jnp.bfloat16)
    count = parts
    up = [(i, i + 1) for i in range(count - 1)]
    down = [(i + 1, i) for i in range(count - 1)]
    prev = lax.ppermute(latent[:, -1], "seq", up)
    nxt = lax.ppermute(latent[:, 0], "seq", down)
    at = lax.broadcasted_iota(jnp.int32, (16, 1), 0)
    halo = jnp.where(at < 8, nxt[None, :], prev[None, :])
    lat = jnp.concatenate([latent.T, halo], axis=0)
    return lat


def body(
    signal,
    gate,
    filter_taps,
    skip,
    up1_weight,
    up1_bias,
    res1_weight,
    res1_bias,
    up2_weight,
    up2_bias,
    res2_weight,
    res2_bias,
    up3_weight,
    up3_bias,
    res3_weight,
    res3_bias,
):
    parts, groups = lax.axis_size("seq"), lax.axis_size("grp")
    chans, frames = signal.shape
    if frames == 128 and parts % 2 == 0 and chans % (groups * parts * 16) == 0:
        first_lag = (lax.broadcasted_iota(jnp.int32, (1, frames), 1) == 0) & (lax.axis_index("seq") == 0)
        taps = (filter_taps + jnp.where(first_lag, skip[:, None], 0.0)).astype(jnp.bfloat16)
        lat = mix(signal, gate, taps, groups, parts)
    else:
        lat = transformed(signal, gate, filter_taps, skip)
    me = lax.axis_index("seq")
    weights = (
        up1_weight, up1_bias, res1_weight, res1_bias, up2_weight, up2_bias,
        res2_weight, res2_bias, up3_weight, up3_bias, res3_weight, res3_bias,
    )
    return decode(lat, me == 0, me == parts - 1, weights)


def solution(mesh):
    placed = (
        P(None, ("grp", "seq")),
        P(None, ("grp", "seq")),
        P(None, "seq"),
        P(),
        P(),
        P(),
        P(),
        P(),
        P(),
        P(),
        P(),
        P(),
        P(),
        P(),
        P(),
        P(),
    )
    return jax.shard_map(
        body, mesh=mesh, in_specs=placed, out_specs=P(("grp", "seq"), None), check_vma=False
    )
```

```python
import functools
import math

import jax
import jax.numpy as jnp
from jax import lax
from jax.experimental import pallas as pl
from jax.experimental.pallas import tpu as pltpu
from jax.sharding import PartitionSpec as P

HIGHEST = lax.Precision.HIGHEST


def angle_table(rows, cols, modulus):
    product = (
        lax.broadcasted_iota(jnp.int32, (rows, cols), 0)
        * lax.broadcasted_iota(jnp.int32, (rows, cols), 1)
        % modulus
    )
    theta = product.astype(jnp.float32) * (2.0 * math.pi / modulus)
    return (jnp.cos(theta), jnp.sin(theta))


def forward(values, tables):
    outer_cos, outer_sin, twist_cos, twist_sin, inner_cos, inner_sin = tables
    first_re = jnp.einsum("kn,cnm->ckm", outer_cos, values, precision=HIGHEST)
    first_im = -jnp.einsum("kn,cnm->ckm", outer_sin, values, precision=HIGHEST)
    turned_re = first_re * twist_cos + first_im * twist_sin
    turned_im = first_im * twist_cos - first_re * twist_sin
    spec_re = jnp.einsum("ckm,mj->ckj", turned_re, inner_cos, precision=HIGHEST) + jnp.einsum(
        "ckm,mj->ckj", turned_im, inner_sin, precision=HIGHEST
    )
    spec_im = jnp.einsum("ckm,mj->ckj", turned_im, inner_cos, precision=HIGHEST) - jnp.einsum(
        "ckm,mj->ckj", turned_re, inner_sin, precision=HIGHEST
    )
    return (spec_re, spec_im)


def inverse(spec_re, spec_im, tables, modulus):
    outer_cos, outer_sin, twist_cos, twist_sin, inner_cos, inner_sin = tables
    back_re = jnp.einsum("ckm,mj->ckj", spec_re, inner_cos, precision=HIGHEST) - jnp.einsum(
        "ckm,mj->ckj", spec_im, inner_sin, precision=HIGHEST
    )
    back_im = jnp.einsum("ckm,mj->ckj", spec_im, inner_cos, precision=HIGHEST) + jnp.einsum(
        "ckm,mj->ckj", spec_re, inner_sin, precision=HIGHEST
    )
    turned_re = back_re * twist_cos - back_im * twist_sin
    turned_im = back_im * twist_cos + back_re * twist_sin
    result = jnp.einsum("kn,ckm->cnm", outer_cos, turned_re, precision=HIGHEST) - jnp.einsum(
        "kn,ckm->cnm", outer_sin, turned_im, precision=HIGHEST
    )
    return result / modulus


def gelu(v):
    return 0.5 * v * (1.0 + jnp.tanh(0.7978845608 * (v + 0.044715 * (v * v * v))))


def decoder_kernel(
    frames, edge, lat_ref, b1_ref, rb1_ref, b2_ref, rb2_ref, b3_ref, rb3_ref,
    up1_hbm, res1_hbm, up2_hbm, res2_hbm, up3_hbm, res3_hbm,
    out_ref,
    up1, res1, up2, res2, up3, res3, act1, hid1, x1, act2, hid2, x2, act3, hid3, fine, sems,
):
    w1, w2, w3 = b1_ref.shape[1], b2_ref.shape[1], b3_ref.shape[1]
    copies = [
        pltpu.make_async_copy(src, dst, sems.at[i])
        for i, (src, dst) in enumerate(
            [
                (up1_hbm, up1),
                (res1_hbm, res1),
                (up2_hbm, up2),
                (res2_hbm, res2),
                (up3_hbm, up3),
                (res3_hbm, res3.at[pl.ds(0, 7 * w3), pl.ds(0, w3)]),
                (res3_hbm, res3.at[pl.ds(w3, 7 * w3), pl.ds(w3, w3)]),
            ]
        )
    ]
    for copy in copies:
        copy.start()
    res3[7 * w3 : 8 * w3, 0:w3] = jnp.zeros((w3, w3), res3.dtype)
    res3[0:w3, w3 : 2 * w3] = jnp.zeros((w3, w3), res3.dtype)
    rows = frames + edge
    at = lax.broadcasted_iota(jnp.int32, (rows, 1), 0)
    me, parts = lax.axis_index("seq"), lax.axis_size("seq")
    keep_first = jnp.where(me == 0, 0.0, 1.0)
    keep_last = jnp.where(me == parts - 1, 0.0, 1.0)
    before_scale = jnp.where(at == 0, keep_first, 1.0)
    after_scale = jnp.where(at == frames - 1, keep_last, 1.0)

    def before(v):
        return (pltpu.roll(v, 1, 0) * before_scale).astype(jnp.bfloat16)

    def after(v):
        return (pltpu.roll(v, rows - 1, 0) * after_scale).astype(jnp.bfloat16)

    def dot(a, b):
        return jnp.dot(a, b, preferred_element_type=jnp.float32)

    copies[0].wait()
    for k in range(4):
        h = (dot(lat_ref[...], up1[:, k * w1 : (k + 1) * w1]) + b1_ref[...]).astype(jnp.bfloat16)
        hid1[:, k * w1 : (k + 1) * w1] = h
        a = gelu(h.astype(jnp.float32))
        act1[:, (3 + k) * w1 : (4 + k) * w1] = a.astype(jnp.bfloat16)
        if k > 0:
            act1[:, (k - 1) * w1 : k * w1] = before(a)
        if k < 3:
            act1[:, (7 + k) * w1 : (8 + k) * w1] = after(a)
    copies[1].wait()
    for k in range(4):
        y = dot(act1[:, k * w1 : (k + 7) * w1], res1[...])
        y = y + hid1[:, k * w1 : (k + 1) * w1].astype(jnp.float32) + rb1_ref[...]
        x1[k * rows : (k + 1) * rows, :] = y.astype(jnp.bfloat16)

    def section(blocks, x, up, up_bias, hid, act, w, group):
        @pl.loop(0, blocks)
        def _(b):
            here = pl.ds(pl.multiple_of(b * rows, 16), rows)
            prev = pl.ds(pl.multiple_of(lax.rem(b + blocks - 1, blocks) * rows, 16), rows)
            nxt = pl.ds(pl.multiple_of(lax.rem(b + 1, blocks) * rows, 16), rows)
            h = (dot(x[here, :], up[...]) + jnp.concatenate([up_bias[...]] * 4, axis=1)).astype(jnp.bfloat16)
            hid[here, :] = h
            a = gelu(h.astype(jnp.float32))
            low = a.astype(jnp.bfloat16)
            act[here, 3 * w : 7 * w] = low

            @pl.when(b < blocks - 1)
            def _():
                act[nxt, 0 : 3 * w] = low[:, w:]

            @pl.when(b == blocks - 1)
            def _():
                act[0:rows, 0 : 3 * w] = before(a[:, w:])

            @pl.when(b > 0)
            def _():
                act[prev, 7 * w : 10 * w] = low[:, : 3 * w]

            @pl.when(b == 0)
            def _():
                act[(blocks - 1) * rows : blocks * rows, 7 * w : 10 * w] = after(a[:, : 3 * w])

    copies[2].wait()
    section(4, x1, up2, b2_ref, hid2, act2, w2, 1)
    copies[3].wait()

    for k in range(4):
        @pl.loop(0, 2)
        def _(b):
            here = pl.ds(pl.multiple_of(b * 2 * rows, 16), 2 * rows)
            y = dot(act2[here, k * w2 : (k + 7) * w2], res2[...])
            y = (y + hid2[here, k * w2 : (k + 1) * w2].astype(jnp.float32) + rb2_ref[...]).astype(jnp.bfloat16)
            for i in range(2):
                x2[pl.ds(pl.multiple_of((b * 8 + i * 4 + k) * rows, 16), rows), :] = y[i * rows : (i + 1) * rows]

    copies[4].wait()
    section(16, x2, up3, b3_ref, hid3, act3, w3, 1)
    copies[5].wait()
    copies[6].wait()
    rb3 = jnp.concatenate([rb3_ref[...]] * 2, axis=1)

    @pl.loop(0, 16)
    def _(b):
        here = pl.ds(pl.multiple_of(b * rows, 16), frames)
        for k in range(2):
            y = dot(act3[here, 2 * k * w3 : (2 * k + 8) * w3], res3[...])
            y = y + hid3[here, 2 * k * w3 : (2 * k + 2) * w3].astype(jnp.float32) + rb3
            for i in range(2):
                fine[pl.ds(b * 4 + 2 * k + i, frames, stride=64), :] = y[:, i * w3 : (i + 1) * w3]

    @pl.loop(0, 16)
    def _(b):
        here = pl.ds(pl.multiple_of(b * 4 * frames, 16), 4 * frames)
        out_ref[here, :] = fine[here, :].astype(jnp.bfloat16)


def decode(lat, weights):
    (up1, b1, res1, rb1, up2, b2, res2, rb2, up3, b3, res3, rb3) = weights
    rows = lat.shape[0]
    edge = 16
    frames = rows - edge
    w1, w2, w3 = b1.shape[0], b2.shape[0], b3.shape[0]
    row = lambda v: v[None, :]
    vm = pl.BlockSpec(memory_space=pltpu.VMEM)
    hb = pl.BlockSpec(memory_space=pl.ANY)
    bf = jnp.bfloat16
    return pl.pallas_call(
        functools.partial(decoder_kernel, frames, edge),
        out_shape=jax.ShapeDtypeStruct((frames * 64, w3), bf),
        in_specs=[vm] * 7 + [hb] * 6,
        out_specs=vm,
        scratch_shapes=[
            pltpu.VMEM(up1.shape, bf),
            pltpu.VMEM(res1.shape, bf),
            pltpu.VMEM(up2.shape, bf),
            pltpu.VMEM(res2.shape, bf),
            pltpu.VMEM(up3.shape, bf),
            pltpu.VMEM((8 * w3, 2 * w3), bf),
            pltpu.VMEM((rows, 10 * w1), bf),
            pltpu.VMEM((rows, 4 * w1), bf),
            pltpu.VMEM((4 * rows, w1), bf),
            pltpu.VMEM((4 * rows, 10 * w2), bf),
            pltpu.VMEM((4 * rows, 4 * w2), bf),
            pltpu.VMEM((16 * rows, w2), bf),
            pltpu.VMEM((16 * rows, 10 * w3), bf),
            pltpu.VMEM((16 * rows, 4 * w3), bf),
            pltpu.VMEM((64 * frames, w3), jnp.float32),
            pltpu.SemaphoreType.DMA((7,)),
        ],
        compiler_params=pltpu.CompilerParams(vmem_limit_bytes=60 * 1024 * 1024),
    )(lat, row(b1), row(rb1), row(b2), row(rb2), row(b3), row(rb3), up1, res1, up2, res2, up3, res3)


CHUNKS = 2


def mix_kernel(
    groups, parts, nc, sig_ref, gate_hbm, tap_ref, lat_ref, gate_ref,
    sig_in, tap_in, mix_out, mix_in, tap_wide, sig_wide, mix_wide, line, edge_next, edge_prev,
    sig_send, sig_recv, tap_send, tap_recv, mix_send, mix_recv, edge_send, edge_recv, own_sem,
):
    g, s = lax.axis_index("grp"), lax.axis_index("seq")
    total = groups * parts
    me = g * parts + s
    frames = sig_ref.shape[1]

    def place(index):
        return (index // parts, lax.rem(index, parts))

    half = nc // CHUNKS

    def rows(index, q):
        return pl.ds(pl.multiple_of(index * nc + q * half, 16), half)

    def slots(index, q, count):
        return pl.ds(pl.multiple_of((q * count + index) * half, 16), half)

    def sig_copy(peer, slot, q):
        return pltpu.make_async_remote_copy(
            sig_ref.at[rows(peer, q)], sig_in.at[slots(slot, q, total)],
            sig_send.at[q * total + peer], sig_recv.at[q * total + slot],
            device_id=place(peer), device_id_type=pl.DeviceIdType.MESH,
        )

    def tap_copy(peer, slot, q):
        return pltpu.make_async_remote_copy(
            tap_ref.at[rows(g * parts + peer, q)], tap_in.at[slots(slot, q, parts)],
            tap_send.at[q * parts + peer], tap_recv.at[q * parts + slot],
            device_id=(g, peer), device_id_type=pl.DeviceIdType.MESH,
        )

    def mix_copy(peer, slot, q):
        return pltpu.make_async_remote_copy(
            mix_out.at[slots(peer, q, total)], mix_in.at[rows(slot, q)],
            mix_send.at[q * total + peer], mix_recv.at[q * total + slot],
            device_id=place(peer), device_id_type=pl.DeviceIdType.MESH,
        )

    own = [pltpu.make_async_copy(gate_hbm, gate_ref, own_sem.at[CHUNKS])]
    for q in range(CHUNKS):
        own.append(
            pltpu.make_async_copy(sig_ref.at[rows(me, q)], sig_in.at[slots(me, q, total)], own_sem.at[q])
        )
    for copy in own:
        copy.start()
    barrier = pltpu.get_barrier_semaphore()

    @pl.loop(1, total)
    def _(step):
        pl.semaphore_signal(
            barrier, inc=1, device_id=place(lax.rem(me + step, total)), device_id_type=pl.DeviceIdType.MESH
        )

    pl.semaphore_wait(barrier, total - 1)

    for q in range(CHUNKS):
        @pl.loop(1, parts)
        def _(step):
            tap_copy(lax.rem(s + step, parts), s, q).start()

        @pl.loop(1, total)
        def _(step):
            sig_copy(lax.rem(me + step, total), me, q).start()

        tap_in[slots(s, q, parts), :] = tap_ref[rows(me, q), :]

    line[...] = jnp.zeros_like(line)
    below = lax.broadcasted_iota(jnp.int32, (frames, frames), 1) >= lax.broadcasted_iota(
        jnp.int32, (frames, frames), 0
    )

    for q in range(CHUNKS):
        @pl.loop(1, parts)
        def _(step):
            tap_copy(s, lax.rem(s + step, parts), q).wait_recv()

        few = slice(q * parts * half, (q + 1) * parts * half)
        tap_wide[few, :] = tap_in[few, :].astype(jnp.float32)
        own[1 + q].wait()

        @pl.loop(1, total)
        def _(step):
            sig_copy(me, lax.rem(me + step, total), q).wait_recv()

        many = slice(q * total * half, (q + 1) * total * half)
        sig_wide[many, :] = sig_in[many, :].astype(jnp.float32)

        @pl.loop(0, half)
        def _(c):
            for part in range(groups):
                line[(2 * part + 1) * parts : (2 * part + 2) * parts, :] = sig_wide[
                    pl.ds((q * total + part * parts) * half + c, parts, stride=half), :
                ]
            acc = jnp.zeros((total, frames), jnp.float32)
            last = jnp.zeros((frames, frames), jnp.float32)
            for pair in range(0, parts, 2):
                tiles, shifted = [], []
                for d in (pair, pair + 1):
                    row = tap_wide[pl.ds((q * parts + d) * half + c, 1), :]
                    turned = pltpu.roll(jnp.broadcast_to(row, (frames, frames)), 0, 1, stride=1, stride_axis=0)
                    tiles.append(jnp.where(below, turned, last).astype(jnp.bfloat16))
                    last = turned
                    shifted.append(
                        jnp.concatenate(
                            [
                                line[(2 * part + 1) * parts - d : (2 * part + 2) * parts - d, :]
                                for part in range(groups)
                            ],
                            axis=0,
                        ).astype(jnp.bfloat16)
                    )
                acc = acc + jnp.dot(
                    jnp.concatenate(shifted, axis=1),
                    jnp.concatenate(tiles, axis=0),
                    preferred_element_type=jnp.float32,
                )
            mix_wide[pl.ds(q * total * half + c, total, stride=half), :] = acc

        mix_out[many, :] = mix_wide[many, :].astype(jnp.bfloat16)

        @pl.loop(1, total)
        def _(step):
            mix_copy(lax.rem(me + step, total), me, q).start()

        mix_in[rows(me, q), :] = mix_out[slots(me, q, total), :]

    own[0].wait()
    for q in range(CHUNKS):
        @pl.loop(1, total)
        def _(step):
            mix_copy(me, lax.rem(me + step, total), q).wait_recv()

    latent = mix_in[...].astype(jnp.float32) * gate_ref[...].astype(jnp.float32)
    lat_ref[0:frames, :] = latent.T.astype(jnp.bfloat16)

    nxt, prv = lax.rem(s + 1, parts), lax.rem(s + parts - 1, parts)
    down = pltpu.make_async_remote_copy(
        lat_ref.at[pl.ds(0, 16)], edge_next, edge_send.at[0], edge_recv.at[0],
        device_id=(g, prv), device_id_type=pl.DeviceIdType.MESH,
    )
    up = pltpu.make_async_remote_copy(
        lat_ref.at[pl.ds(frames - 16, 16)], edge_prev, edge_send.at[1], edge_recv.at[1],
        device_id=(g, nxt), device_id_type=pl.DeviceIdType.MESH,
    )
    down.start()
    up.start()

    for q in range(CHUNKS):
        @pl.loop(1, parts)
        def _(step):
            tap_copy(lax.rem(s + step, parts), s, q).wait_send()

        @pl.loop(1, total)
        def _(step):
            sig_copy(lax.rem(me + step, total), me, q).wait_send()
            mix_copy(lax.rem(me + step, total), me, q).wait_send()

    down.wait()
    up.wait()
    at = lax.broadcasted_iota(jnp.int32, (16, 1), 0)
    lat_ref[frames : frames + 16, :] = jnp.where(
        at < 8, edge_next[...].astype(jnp.float32), edge_prev[...].astype(jnp.float32)
    ).astype(jnp.bfloat16)


def mix(signal, gate, taps, groups, parts):
    chans, frames = signal.shape
    total = groups * parts
    nc = chans // total
    hb = pl.BlockSpec(memory_space=pl.ANY)
    vm = pl.BlockSpec(memory_space=pltpu.VMEM)
    bf, f32 = jnp.bfloat16, jnp.float32
    dma = pltpu.SemaphoreType.DMA
    return pl.pallas_call(
        functools.partial(mix_kernel, groups, parts, nc),
        out_shape=jax.ShapeDtypeStruct((frames + 16, chans), bf),
        in_specs=[hb, hb, vm],
        out_specs=vm,
        scratch_shapes=[
            pltpu.VMEM((chans, frames), bf),
            pltpu.VMEM((chans, frames), bf),
            pltpu.VMEM((parts * nc, frames), bf),
            pltpu.VMEM((chans, frames), bf),
            pltpu.VMEM((chans, frames), bf),
            pltpu.VMEM((parts * nc, frames), f32),
            pltpu.VMEM((chans, frames), f32),
            pltpu.VMEM((chans, frames), f32),
            pltpu.VMEM((groups * 2 * parts, frames), f32),
            pltpu.VMEM((16, chans), bf),
            pltpu.VMEM((16, chans), bf),
            dma((CHUNKS * total,)), dma((CHUNKS * total,)), dma((CHUNKS * parts,)), dma((CHUNKS * parts,)),
            dma((CHUNKS * total,)), dma((CHUNKS * total,)), dma((2,)), dma((2,)), dma((CHUNKS + 1,)),
        ],
        compiler_params=pltpu.CompilerParams(
            collective_id=0, has_side_effects=True, vmem_limit_bytes=40 * 1024 * 1024
        ),
    )(signal, gate, taps)


def transformed(signal, gate, filter_taps, skip):
    parts = lax.axis_size("seq")
    frames = signal.shape[1]
    chans = signal.shape[0] // parts
    modulus = 2 * parts * frames
    source, taps = (
        lax.all_to_all(
            signal.astype(jnp.float32).astype(jnp.bfloat16),
            "seq",
            split_axis=0,
            concat_axis=1,
            tiled=True,
        ).astype(jnp.float32),
        lax.all_to_all(
            filter_taps.astype(jnp.bfloat16), "seq", split_axis=0, concat_axis=1, tiled=True
        ).astype(filter_taps.dtype),
    )
    my_skip = lax.dynamic_slice_in_dim(skip, lax.axis_index("seq") * chans, chans, 0)
    tables = (
        angle_table(2 * parts, parts, 2 * parts)
        + angle_table(2 * parts, frames, modulus)
        + angle_table(frames, frames, frames)
    )
    sig_re, sig_im = forward(source.reshape(chans, parts, frames), tables)
    fil_re, fil_im = forward(taps.reshape(chans, parts, frames), tables)
    prod_re = sig_re * fil_re - sig_im * fil_im
    prod_im = sig_re * fil_im + sig_im * fil_re
    conv = inverse(prod_re, prod_im, tables, modulus).reshape(chans, parts * frames)
    mixed = (conv + my_skip[:, None] * source).astype(jnp.bfloat16)
    arrived = lax.all_to_all(mixed, "seq", split_axis=1, concat_axis=0, tiled=True)
    latent = (gate.astype(jnp.float32) * arrived.astype(jnp.float32)).astype(jnp.bfloat16)
    count = parts
    up = [(i, i + 1) for i in range(count - 1)]
    down = [(i + 1, i) for i in range(count - 1)]
    prev = lax.ppermute(latent[:, -1], "seq", up)
    nxt = lax.ppermute(latent[:, 0], "seq", down)
    at = lax.broadcasted_iota(jnp.int32, (16, 1), 0)
    halo = jnp.where(at < 8, nxt[None, :], prev[None, :])
    lat = jnp.concatenate([latent.T, halo], axis=0)
    return lat


def body(
    signal,
    gate,
    filter_taps,
    skip,
    up1_weight,
    up1_bias,
    res1_weight,
    res1_bias,
    up2_weight,
    up2_bias,
    res2_weight,
    res2_bias,
    up3_weight,
    up3_bias,
    res3_weight,
    res3_bias,
):
    parts, groups = lax.axis_size("seq"), lax.axis_size("grp")
    chans, frames = signal.shape
    if frames == 128 and parts % 2 == 0 and chans % (groups * parts * 16 * CHUNKS) == 0:
        first_lag = (lax.broadcasted_iota(jnp.int32, (1, frames), 1) == 0) & (lax.axis_index("seq") == 0)
        taps = (filter_taps + jnp.where(first_lag, skip[:, None], 0.0)).astype(jnp.bfloat16)
        lat = mix(signal, gate, taps, groups, parts)
    else:
        lat = transformed(signal, gate, filter_taps, skip)
    weights = (
        up1_weight, up1_bias, res1_weight, res1_bias, up2_weight, up2_bias,
        res2_weight, res2_bias, up3_weight, up3_bias, res3_weight, res3_bias,
    )
    return decode(lat, weights)


def solution(mesh):
    placed = (
        P(None, ("grp", "seq")),
        P(None, ("grp", "seq")),
        P(None, "seq"),
        P(),
        P(),
        P(),
        P(),
        P(),
        P(),
        P(),
        P(),
        P(),
        P(),
        P(),
        P(),
        P(),
    )
    return jax.shard_map(
        body, mesh=mesh, in_specs=placed, out_specs=P(("grp", "seq"), None), check_vma=False
    )
```

```python
import functools
import math

import jax
import jax.numpy as jnp
from jax import lax
from jax.experimental import pallas as pl
from jax.experimental.pallas import tpu as pltpu
from jax.sharding import PartitionSpec as P

HIGHEST = lax.Precision.HIGHEST


def angle_table(rows, cols, modulus):
    product = (
        lax.broadcasted_iota(jnp.int32, (rows, cols), 0)
        * lax.broadcasted_iota(jnp.int32, (rows, cols), 1)
        % modulus
    )
    theta = product.astype(jnp.float32) * (2.0 * math.pi / modulus)
    return (jnp.cos(theta), jnp.sin(theta))


def forward(values, tables):
    outer_cos, outer_sin, twist_cos, twist_sin, inner_cos, inner_sin = tables
    first_re = jnp.einsum("kn,cnm->ckm", outer_cos, values, precision=HIGHEST)
    first_im = -jnp.einsum("kn,cnm->ckm", outer_sin, values, precision=HIGHEST)
    turned_re = first_re * twist_cos + first_im * twist_sin
    turned_im = first_im * twist_cos - first_re * twist_sin
    spec_re = jnp.einsum("ckm,mj->ckj", turned_re, inner_cos, precision=HIGHEST) + jnp.einsum(
        "ckm,mj->ckj", turned_im, inner_sin, precision=HIGHEST
    )
    spec_im = jnp.einsum("ckm,mj->ckj", turned_im, inner_cos, precision=HIGHEST) - jnp.einsum(
        "ckm,mj->ckj", turned_re, inner_sin, precision=HIGHEST
    )
    return (spec_re, spec_im)


def inverse(spec_re, spec_im, tables, modulus):
    outer_cos, outer_sin, twist_cos, twist_sin, inner_cos, inner_sin = tables
    back_re = jnp.einsum("ckm,mj->ckj", spec_re, inner_cos, precision=HIGHEST) - jnp.einsum(
        "ckm,mj->ckj", spec_im, inner_sin, precision=HIGHEST
    )
    back_im = jnp.einsum("ckm,mj->ckj", spec_im, inner_cos, precision=HIGHEST) + jnp.einsum(
        "ckm,mj->ckj", spec_re, inner_sin, precision=HIGHEST
    )
    turned_re = back_re * twist_cos - back_im * twist_sin
    turned_im = back_im * twist_cos + back_re * twist_sin
    result = jnp.einsum("kn,ckm->cnm", outer_cos, turned_re, precision=HIGHEST) - jnp.einsum(
        "kn,ckm->cnm", outer_sin, turned_im, precision=HIGHEST
    )
    return result / modulus


def gelu(v):
    return 0.5 * v * (1.0 + jnp.tanh(0.7978845608 * (v + 0.044715 * (v * v * v))))


def decoder_kernel(
    frames, edge, lat_ref, b1_ref, rb1_ref, b2_ref, rb2_ref, b3_ref, rb3_ref,
    up1_hbm, res1_hbm, up2_hbm, res2_hbm, up3_hbm, res3_hbm,
    out_ref,
    up1, res1, up2, res2, up3, res3, act1, hid1, x1, act2, hid2, x2, act3, hid3, fine, sems,
):
    w1, w2, w3 = b1_ref.shape[1], b2_ref.shape[1], b3_ref.shape[1]
    copies = [
        pltpu.make_async_copy(src, dst, sems.at[i])
        for i, (src, dst) in enumerate(
            [
                (up1_hbm, up1),
                (res1_hbm, res1),
                (up2_hbm, up2),
                (res2_hbm, res2),
                (up3_hbm, up3),
                (res3_hbm, res3.at[pl.ds(0, 7 * w3), pl.ds(0, w3)]),
                (res3_hbm, res3.at[pl.ds(w3, 7 * w3), pl.ds(w3, w3)]),
            ]
        )
    ]
    for copy in copies:
        copy.start()
    res3[7 * w3 : 8 * w3, 0:w3] = jnp.zeros((w3, w3), res3.dtype)
    res3[0:w3, w3 : 2 * w3] = jnp.zeros((w3, w3), res3.dtype)
    rows = frames + edge
    at = lax.broadcasted_iota(jnp.int32, (rows, 1), 0)
    me, parts = lax.axis_index("seq"), lax.axis_size("seq")
    keep_first = jnp.where(me == 0, 0.0, 1.0)
    keep_last = jnp.where(me == parts - 1, 0.0, 1.0)
    before_scale = jnp.where(at == 0, keep_first, 1.0)
    after_scale = jnp.where(at == frames - 1, keep_last, 1.0)

    def before(v):
        return (pltpu.roll(v, 1, 0) * before_scale).astype(jnp.bfloat16)

    def after(v):
        return (pltpu.roll(v, rows - 1, 0) * after_scale).astype(jnp.bfloat16)

    def dot(a, b):
        return jnp.dot(a, b, preferred_element_type=jnp.float32)

    copies[0].wait()
    for k in range(4):
        h = (dot(lat_ref[...], up1[:, k * w1 : (k + 1) * w1]) + b1_ref[...]).astype(jnp.bfloat16)
        hid1[:, k * w1 : (k + 1) * w1] = h
        a = gelu(h.astype(jnp.float32))
        act1[:, (3 + k) * w1 : (4 + k) * w1] = a.astype(jnp.bfloat16)
        if k > 0:
            act1[:, (k - 1) * w1 : k * w1] = before(a)
        if k < 3:
            act1[:, (7 + k) * w1 : (8 + k) * w1] = after(a)
    copies[1].wait()
    for k in range(4):
        y = dot(act1[:, k * w1 : (k + 7) * w1], res1[...])
        y = y + hid1[:, k * w1 : (k + 1) * w1].astype(jnp.float32) + rb1_ref[...]
        x1[k * rows : (k + 1) * rows, :] = y.astype(jnp.bfloat16)

    def section(blocks, x, up, up_bias, hid, act, w, group):
        @pl.loop(0, blocks, unroll=2)
        def _(b):
            here = pl.ds(pl.multiple_of(b * rows, 16), rows)
            prev = pl.ds(pl.multiple_of(lax.rem(b + blocks - 1, blocks) * rows, 16), rows)
            nxt = pl.ds(pl.multiple_of(lax.rem(b + 1, blocks) * rows, 16), rows)
            h = (dot(x[here, :], up[...]) + jnp.concatenate([up_bias[...]] * 4, axis=1)).astype(jnp.bfloat16)
            hid[here, :] = h
            a = gelu(h.astype(jnp.float32))
            low = a.astype(jnp.bfloat16)
            act[here, 3 * w : 7 * w] = low

            act[nxt, 0 : 3 * w] = low[:, w:]
            act[prev, 7 * w : 10 * w] = low[:, : 3 * w]

        end = slice((blocks - 1) * rows, blocks * rows)
        act[0:rows, 0 : 3 * w] = before(act[end, 4 * w : 7 * w].astype(jnp.float32))
        act[end, 7 * w : 10 * w] = after(act[0:rows, 3 * w : 6 * w].astype(jnp.float32))

    copies[2].wait()
    section(4, x1, up2, b2_ref, hid2, act2, w2, 1)
    copies[3].wait()

    for k in range(4):
        @pl.loop(0, 2)
        def _(b):
            here = pl.ds(pl.multiple_of(b * 2 * rows, 16), 2 * rows)
            y = dot(act2[here, k * w2 : (k + 7) * w2], res2[...])
            y = (y + hid2[here, k * w2 : (k + 1) * w2].astype(jnp.float32) + rb2_ref[...]).astype(jnp.bfloat16)
            for i in range(2):
                x2[pl.ds(pl.multiple_of((b * 8 + i * 4 + k) * rows, 16), rows), :] = y[i * rows : (i + 1) * rows]

    copies[4].wait()
    section(16, x2, up3, b3_ref, hid3, act3, w3, 1)
    copies[5].wait()
    copies[6].wait()
    rb3 = jnp.concatenate([rb3_ref[...]] * 2, axis=1)

    @pl.loop(0, 16, unroll=2)
    def _(b):
        here = pl.ds(pl.multiple_of(b * rows, 16), frames)
        for k in range(2):
            y = dot(act3[here, 2 * k * w3 : (2 * k + 8) * w3], res3[...])
            y = y + hid3[here, 2 * k * w3 : (2 * k + 2) * w3].astype(jnp.float32) + rb3
            for i in range(2):
                fine[pl.ds(b * 4 + 2 * k + i, frames, stride=64), :] = y[:, i * w3 : (i + 1) * w3]

    @pl.loop(0, 16, unroll=2)
    def _(b):
        here = pl.ds(pl.multiple_of(b * 4 * frames, 16), 4 * frames)
        out_ref[here, :] = fine[here, :].astype(jnp.bfloat16)


def decode(lat, weights):
    (up1, b1, res1, rb1, up2, b2, res2, rb2, up3, b3, res3, rb3) = weights
    rows = lat.shape[0]
    edge = 16
    frames = rows - edge
    w1, w2, w3 = b1.shape[0], b2.shape[0], b3.shape[0]
    row = lambda v: v[None, :]
    vm = pl.BlockSpec(memory_space=pltpu.VMEM)
    hb = pl.BlockSpec(memory_space=pl.ANY)
    bf = jnp.bfloat16
    return pl.pallas_call(
        functools.partial(decoder_kernel, frames, edge),
        out_shape=jax.ShapeDtypeStruct((frames * 64, w3), bf),
        in_specs=[vm] * 7 + [hb] * 6,
        out_specs=vm,
        scratch_shapes=[
            pltpu.VMEM(up1.shape, bf),
            pltpu.VMEM(res1.shape, bf),
            pltpu.VMEM(up2.shape, bf),
            pltpu.VMEM(res2.shape, bf),
            pltpu.VMEM(up3.shape, bf),
            pltpu.VMEM((8 * w3, 2 * w3), bf),
            pltpu.VMEM((rows, 10 * w1), bf),
            pltpu.VMEM((rows, 4 * w1), bf),
            pltpu.VMEM((4 * rows, w1), bf),
            pltpu.VMEM((4 * rows, 10 * w2), bf),
            pltpu.VMEM((4 * rows, 4 * w2), bf),
            pltpu.VMEM((16 * rows, w2), bf),
            pltpu.VMEM((16 * rows, 10 * w3), bf),
            pltpu.VMEM((16 * rows, 4 * w3), bf),
            pltpu.VMEM((64 * frames, w3), jnp.float32),
            pltpu.SemaphoreType.DMA((7,)),
        ],
        compiler_params=pltpu.CompilerParams(vmem_limit_bytes=60 * 1024 * 1024),
    )(lat, row(b1), row(rb1), row(b2), row(rb2), row(b3), row(rb3), up1, res1, up2, res2, up3, res3)


CHUNKS = 2


def mix_kernel(
    groups, parts, nc, sig_ref, gate_hbm, tap_ref, lat_ref, gate_ref,
    sig_in, tap_in, mix_out, mix_in, tap_wide, sig_wide, mix_wide, line, edge_next, edge_prev,
    sig_send, sig_recv, tap_send, tap_recv, mix_send, mix_recv, edge_send, edge_recv, own_sem,
):
    g, s = lax.axis_index("grp"), lax.axis_index("seq")
    total = groups * parts
    me = g * parts + s
    frames = sig_ref.shape[1]

    def place(index):
        return (index // parts, lax.rem(index, parts))

    half = nc // CHUNKS

    def rows(index, q):
        return pl.ds(pl.multiple_of(index * nc + q * half, 16), half)

    def slots(index, q, count):
        return pl.ds(pl.multiple_of((q * count + index) * half, 16), half)

    def sig_copy(peer, slot, q):
        return pltpu.make_async_remote_copy(
            sig_ref.at[rows(peer, q)], sig_in.at[slots(slot, q, total)],
            sig_send.at[q * total + peer], sig_recv.at[q * total + slot],
            device_id=place(peer), device_id_type=pl.DeviceIdType.MESH,
        )

    def tap_copy(peer, slot, q):
        return pltpu.make_async_remote_copy(
            tap_ref.at[rows(g * parts + peer, q)], tap_in.at[slots(slot, q, parts)],
            tap_send.at[q * parts + peer], tap_recv.at[q * parts + slot],
            device_id=(g, peer), device_id_type=pl.DeviceIdType.MESH,
        )

    def mix_copy(peer, slot, q):
        return pltpu.make_async_remote_copy(
            mix_out.at[slots(peer, q, total)], mix_in.at[rows(slot, q)],
            mix_send.at[q * total + peer], mix_recv.at[q * total + slot],
            device_id=place(peer), device_id_type=pl.DeviceIdType.MESH,
        )

    own = [pltpu.make_async_copy(gate_hbm, gate_ref, own_sem.at[CHUNKS])]
    for q in range(CHUNKS):
        own.append(
            pltpu.make_async_copy(sig_ref.at[rows(me, q)], sig_in.at[slots(me, q, total)], own_sem.at[q])
        )
    for copy in own:
        copy.start()
    barrier = pltpu.get_barrier_semaphore()

    @pl.loop(1, total)
    def _(step):
        pl.semaphore_signal(
            barrier, inc=1, device_id=place(lax.rem(me + step, total)), device_id_type=pl.DeviceIdType.MESH
        )

    pl.semaphore_wait(barrier, total - 1)

    for q in range(CHUNKS):
        @pl.loop(1, parts)
        def _(step):
            tap_copy(lax.rem(s + step, parts), s, q).start()

        @pl.loop(1, total)
        def _(step):
            sig_copy(lax.rem(me + step, total), me, q).start()

        tap_in[slots(s, q, parts), :] = tap_ref[rows(me, q), :]

    line[...] = jnp.zeros_like(line)
    below = lax.broadcasted_iota(jnp.int32, (frames, frames), 1) >= lax.broadcasted_iota(
        jnp.int32, (frames, frames), 0
    )

    for q in range(CHUNKS):
        @pl.loop(1, parts)
        def _(step):
            tap_copy(s, lax.rem(s + step, parts), q).wait_recv()

        few = slice(q * parts * half, (q + 1) * parts * half)
        tap_wide[few, :] = tap_in[few, :].astype(jnp.float32)
        own[1 + q].wait()

        @pl.loop(1, total)
        def _(step):
            sig_copy(me, lax.rem(me + step, total), q).wait_recv()

        many = slice(q * total * half, (q + 1) * total * half)
        sig_wide[many, :] = sig_in[many, :].astype(jnp.float32)

        @pl.loop(0, half)
        def _(c):
            for part in range(groups):
                line[(2 * part + 1) * parts : (2 * part + 2) * parts, :] = sig_wide[
                    pl.ds((q * total + part * parts) * half + c, parts, stride=half), :
                ]
            acc = jnp.zeros((total, frames), jnp.float32)
            last = jnp.zeros((frames, frames), jnp.float32)
            for pair in range(0, parts, 2):
                tiles, shifted = [], []
                for d in (pair, pair + 1):
                    row = tap_wide[pl.ds((q * parts + d) * half + c, 1), :]
                    turned = pltpu.roll(jnp.broadcast_to(row, (frames, frames)), 0, 1, stride=1, stride_axis=0)
                    tiles.append(jnp.where(below, turned, last).astype(jnp.bfloat16))
                    last = turned
                    shifted.append(
                        jnp.concatenate(
                            [
                                line[(2 * part + 1) * parts - d : (2 * part + 2) * parts - d, :]
                                for part in range(groups)
                            ],
                            axis=0,
                        ).astype(jnp.bfloat16)
                    )
                acc = acc + jnp.dot(
                    jnp.concatenate(shifted, axis=1),
                    jnp.concatenate(tiles, axis=0),
                    preferred_element_type=jnp.float32,
                )
            mix_wide[pl.ds(q * total * half + c, total, stride=half), :] = acc

        mix_out[many, :] = mix_wide[many, :].astype(jnp.bfloat16)

        @pl.loop(1, total)
        def _(step):
            mix_copy(lax.rem(me + step, total), me, q).start()

        mix_in[rows(me, q), :] = mix_out[slots(me, q, total), :]

    own[0].wait()
    for q in range(CHUNKS):
        @pl.loop(1, total)
        def _(step):
            mix_copy(me, lax.rem(me + step, total), q).wait_recv()

    latent = mix_in[...].astype(jnp.float32) * gate_ref[...].astype(jnp.float32)
    lat_ref[0:frames, :] = latent.T.astype(jnp.bfloat16)

    nxt, prv = lax.rem(s + 1, parts), lax.rem(s + parts - 1, parts)
    down = pltpu.make_async_remote_copy(
        lat_ref.at[pl.ds(0, 16)], edge_next, edge_send.at[0], edge_recv.at[0],
        device_id=(g, prv), device_id_type=pl.DeviceIdType.MESH,
    )
    up = pltpu.make_async_remote_copy(
        lat_ref.at[pl.ds(frames - 16, 16)], edge_prev, edge_send.at[1], edge_recv.at[1],
        device_id=(g, nxt), device_id_type=pl.DeviceIdType.MESH,
    )
    down.start()
    up.start()

    for q in range(CHUNKS):
        @pl.loop(1, parts)
        def _(step):
            tap_copy(lax.rem(s + step, parts), s, q).wait_send()

        @pl.loop(1, total)
        def _(step):
            sig_copy(lax.rem(me + step, total), me, q).wait_send()
            mix_copy(lax.rem(me + step, total), me, q).wait_send()

    down.wait()
    up.wait()
    at = lax.broadcasted_iota(jnp.int32, (16, 1), 0)
    lat_ref[frames : frames + 16, :] = jnp.where(
        at < 8, edge_next[...].astype(jnp.float32), edge_prev[...].astype(jnp.float32)
    ).astype(jnp.bfloat16)


def mix(signal, gate, taps, groups, parts):
    chans, frames = signal.shape
    total = groups * parts
    nc = chans // total
    hb = pl.BlockSpec(memory_space=pl.ANY)
    vm = pl.BlockSpec(memory_space=pltpu.VMEM)
    bf, f32 = jnp.bfloat16, jnp.float32
    dma = pltpu.SemaphoreType.DMA
    return pl.pallas_call(
        functools.partial(mix_kernel, groups, parts, nc),
        out_shape=jax.ShapeDtypeStruct((frames + 16, chans), bf),
        in_specs=[hb, hb, vm],
        out_specs=vm,
        scratch_shapes=[
            pltpu.VMEM((chans, frames), bf),
            pltpu.VMEM((chans, frames), bf),
            pltpu.VMEM((parts * nc, frames), bf),
            pltpu.VMEM((chans, frames), bf),
            pltpu.VMEM((chans, frames), bf),
            pltpu.VMEM((parts * nc, frames), f32),
            pltpu.VMEM((chans, frames), f32),
            pltpu.VMEM((chans, frames), f32),
            pltpu.VMEM((groups * 2 * parts, frames), f32),
            pltpu.VMEM((16, chans), bf),
            pltpu.VMEM((16, chans), bf),
            dma((CHUNKS * total,)), dma((CHUNKS * total,)), dma((CHUNKS * parts,)), dma((CHUNKS * parts,)),
            dma((CHUNKS * total,)), dma((CHUNKS * total,)), dma((2,)), dma((2,)), dma((CHUNKS + 1,)),
        ],
        compiler_params=pltpu.CompilerParams(
            collective_id=0, has_side_effects=True, vmem_limit_bytes=60 * 1024 * 1024
        ),
    )(signal, gate, taps)


def transformed(signal, gate, filter_taps, skip):
    parts = lax.axis_size("seq")
    frames = signal.shape[1]
    chans = signal.shape[0] // parts
    modulus = 2 * parts * frames
    source, taps = (
        lax.all_to_all(
            signal.astype(jnp.float32).astype(jnp.bfloat16),
            "seq",
            split_axis=0,
            concat_axis=1,
            tiled=True,
        ).astype(jnp.float32),
        lax.all_to_all(
            filter_taps.astype(jnp.bfloat16), "seq", split_axis=0, concat_axis=1, tiled=True
        ).astype(filter_taps.dtype),
    )
    my_skip = lax.dynamic_slice_in_dim(skip, lax.axis_index("seq") * chans, chans, 0)
    tables = (
        angle_table(2 * parts, parts, 2 * parts)
        + angle_table(2 * parts, frames, modulus)
        + angle_table(frames, frames, frames)
    )
    sig_re, sig_im = forward(source.reshape(chans, parts, frames), tables)
    fil_re, fil_im = forward(taps.reshape(chans, parts, frames), tables)
    prod_re = sig_re * fil_re - sig_im * fil_im
    prod_im = sig_re * fil_im + sig_im * fil_re
    conv = inverse(prod_re, prod_im, tables, modulus).reshape(chans, parts * frames)
    mixed = (conv + my_skip[:, None] * source).astype(jnp.bfloat16)
    arrived = lax.all_to_all(mixed, "seq", split_axis=1, concat_axis=0, tiled=True)
    latent = (gate.astype(jnp.float32) * arrived.astype(jnp.float32)).astype(jnp.bfloat16)
    count = parts
    up = [(i, i + 1) for i in range(count - 1)]
    down = [(i + 1, i) for i in range(count - 1)]
    prev = lax.ppermute(latent[:, -1], "seq", up)
    nxt = lax.ppermute(latent[:, 0], "seq", down)
    at = lax.broadcasted_iota(jnp.int32, (16, 1), 0)
    halo = jnp.where(at < 8, nxt[None, :], prev[None, :])
    lat = jnp.concatenate([latent.T, halo], axis=0)
    return lat


def body(
    signal,
    gate,
    filter_taps,
    skip,
    up1_weight,
    up1_bias,
    res1_weight,
    res1_bias,
    up2_weight,
    up2_bias,
    res2_weight,
    res2_bias,
    up3_weight,
    up3_bias,
    res3_weight,
    res3_bias,
):
    parts, groups = lax.axis_size("seq"), lax.axis_size("grp")
    chans, frames = signal.shape
    if frames == 128 and parts % 2 == 0 and chans % (groups * parts * 16 * CHUNKS) == 0:
        first_lag = (lax.broadcasted_iota(jnp.int32, (1, frames), 1) == 0) & (lax.axis_index("seq") == 0)
        taps = (filter_taps + jnp.where(first_lag, skip[:, None], 0.0)).astype(jnp.bfloat16)
        lat = mix(signal, gate, taps, groups, parts)
    else:
        lat = transformed(signal, gate, filter_taps, skip)
    weights = (
        up1_weight, up1_bias, res1_weight, res1_bias, up2_weight, up2_bias,
        res2_weight, res2_bias, up3_weight, up3_bias, res3_weight, res3_bias,
    )
    return decode(lat, weights)


def solution(mesh):
    placed = (
        P(None, ("grp", "seq")),
        P(None, ("grp", "seq")),
        P(None, "seq"),
        P(),
        P(),
        P(),
        P(),
        P(),
        P(),
        P(),
        P(),
        P(),
        P(),
        P(),
        P(),
        P(),
    )
    return jax.shard_map(
        body, mesh=mesh, in_specs=placed, out_specs=P(("grp", "seq"), None), check_vma=False
    )
```
